32 devices in a mesh: dp: 8 (over y, x, core), ctx: 4 (over z).
Axes of the slice: x: 2, y: 2, z: 4, core: 2. Of those that a mesh axis runs over, the one named last changes fastest.
Arguments:
- query: bfloat16 [4096, 4096], P(('dp', 'ctx')), may hold values from -6 to 6
- keys: bfloat16 [4096, 512], P(('dp', 'ctx')), may hold values from -6 to 6
- values: bfloat16 [4096, 512], P(('dp', 'ctx')), may hold values from -6 to 6
- cotangent: bfloat16 [4096, 4096], P(('dp', 'ctx')), may hold values from -6 to 6
- doc_lengths: int32 [64], replicated, may hold values from 1 to 128, 4096 in all
Outputs:
- key_grad: bfloat16 [4096, 512], P(('dp', 'ctx'))
- value_grad: bfloat16 [4096, 512], P(('dp', 'ctx'))
- query_bias_grad: float32 [4096], replicated
- value_bias_grad: float32 [512], replicated
The draws below stay inside these ranges and needn't reach their ends.
Inputs may be any that keep to these rules, and one draw needn't show every extreme that they name: `doc_lengths`: 64 lengths that sum to 4096; the largest is exactly 128.
All inputs are finite; a program needn't handle non-finite values.
Results may differ from the reference program's by a relative error of at most 0.015.
Values may be sent and summed in bfloat16 or wider, within the bound.
No kernel may reach another device: no remote copies, remote signals or barrier semaphores. Data moves between devices by JAX's collectives and lax.ppermute only.
A program may use at most 64 MiB of HBM per device.

```python
import math
import jax
import jax.numpy as jnp
import numpy as np
from jax import lax

HEAD_DIM = 128
Q_HEADS = 32
KV_HEADS = 4
TOK_DEV = 128
SEQ = 4096
DOC_MOST = 128
DOCS = 64
N_CTX = 4


def draw_query(key, part):
    key = jax.random.fold_in(key, 11)
    result = jnp.clip(jax.random.normal(key, (SEQ, Q_HEADS * HEAD_DIM), jnp.float32), -6.0, 6.0)
    return result.astype(jnp.bfloat16)


def draw_keys(key, part):
    key = jax.random.fold_in(key, 23)
    result = jnp.clip(jax.random.normal(key, (SEQ, KV_HEADS * HEAD_DIM), jnp.float32), -6.0, 6.0)
    return result.astype(jnp.bfloat16)


def block_levels(rng, dims, pieces, low, top_value):
    def one(position, parts):
        steps = jax.random.uniform(jax.random.fold_in(jax.random.fold_in(rng, 6), position), (parts,), jnp.float32, low / len(pieces), top_value / len(pieces))
        return jnp.repeat(jnp.exp(steps), dims[position] // parts).reshape((-1,) + (1,) * (len(dims) - position - 1))

    gain = one(*pieces[0])
    for cut in pieces[1:]:
        gain = gain * one(*cut)
    return gain


def profile(amount, total, bound, skew):
    loads = [(1 << 20) // math.isqrt(grade ** skew) + 1 for grade in range(2, amount + 1)]
    spare, holding = total - bound - (amount - 1), [1] * (amount - 1)
    while spare > 0:
        candidates = [i for i in range(amount - 1) if holding[i] < bound]
        pool, left = sum([loads[i] for i in candidates]), spare
        for i in candidates:
            more = min(bound - holding[i], max(1, left * loads[i] // pool), spare)
            holding[i] = holding[i] + more
            spare = spare - more
    return np.array([bound] + holding)


def ragged(key, count, total, bound, skew):
    if count == 2:
        one = jax.random.randint(key, (), max(1, total - bound), min(bound, total - 1) + 1)
        return jnp.stack([one, total - one])
    tallies = jnp.asarray(profile(count, total, bound, skew), jnp.int32)
    pairs = (count - 1) // 2
    giver, sink = tallies[1:1 + 2 * pairs:2], tallies[2:2 + 2 * pairs:2]
    slack = jnp.minimum(giver - 1, bound - sink)
    moved = jax.random.randint(jax.random.fold_in(key, 1), (pairs,), 0, 1 << 20) % (slack + 1)
    tallies = tallies.at[1:1 + 2 * pairs:2].set(giver - moved).at[2:2 + 2 * pairs:2].set(sink + moved)
    return tallies[jax.random.permutation(jax.random.fold_in(key, 2), count)]


def noise(own_key, extent, scale, reach, cuts=(), kind=jnp.bfloat16):
    loudness = block_levels(own_key, extent, cuts, -0.22, 0.18) if cuts else 1.0
    drawn = jax.random.normal(own_key, extent, jnp.float32) * scale * loudness
    return jnp.minimum(jnp.maximum(drawn, -reach), reach).astype(kind)


def setup_inputs(seed: int = 0) -> dict:
    splits = jax.random.split(jax.random.key(seed), 6)
    return {
        "query": draw_query(jax.random.fold_in(splits[5], 71), 0),
        "keys": draw_keys(jax.random.fold_in(splits[5], 71), 0),
        "values": noise(splits[2], (SEQ, KV_HEADS * HEAD_DIM), 1.0, 6.0, ((0, 32),)),
        "cotangent": noise(splits[3], (SEQ, Q_HEADS * HEAD_DIM), 1.0, 6.0, ((0, 32),)),
        "doc_lengths": ragged(splits[4], DOCS, SEQ, DOC_MOST, 2).astype(jnp.int32),
    }


def segment_ids(lengths, positions):
    ends = jnp.cumsum(lengths)
    return jnp.sum((ends[None, :] <= positions[:, None]).astype(jnp.int32), axis=1)


def reference(query, keys, values, cotangent, doc_lengths):
    groups = Q_HEADS // KV_HEADS
    score_scale = HEAD_DIM ** -0.5
    padding = (N_CTX // 4) * TOK_DEV
    window_rows = padding + TOK_DEV
    query = query.reshape(SEQ, KV_HEADS, groups, HEAD_DIM)
    cotangent = cotangent.reshape(SEQ, KV_HEADS, groups, HEAD_DIM)
    keys = keys.reshape(SEQ, KV_HEADS, HEAD_DIM)
    values = values.reshape(SEQ, KV_HEADS, HEAD_DIM)
    positions = jnp.arange(SEQ, dtype=jnp.int32)
    segments = segment_ids(doc_lengths, positions)
    key_pos = jnp.concatenate([jnp.arange(-padding, 0, dtype=jnp.int32), positions])
    key_seg = jnp.concatenate([jnp.full((padding,), -1, jnp.int32), segments])
    keys_pad = jnp.pad(keys.astype(jnp.float32), ((padding, 0), (0, 0), (0, 0)))
    values_pad = jnp.pad(values.astype(jnp.float32), ((padding, 0), (0, 0), (0, 0)))

    def block_step(carry, block):
        key_acc, value_acc, query_acc = carry
        row_start = (block * TOK_DEV).astype(jnp.int32)
        query_blk = lax.dynamic_slice_in_dim(query, row_start, TOK_DEV, 0).astype(jnp.float32)
        grad_blk = lax.dynamic_slice_in_dim(cotangent, row_start, TOK_DEV, 0).astype(jnp.float32)
        key_win = lax.dynamic_slice_in_dim(keys_pad, row_start, window_rows, 0)
        value_win = lax.dynamic_slice_in_dim(values_pad, row_start, window_rows, 0)
        query_pos = row_start + jnp.arange(TOK_DEV, dtype=jnp.int32)
        query_seg = lax.dynamic_slice_in_dim(segments, row_start, TOK_DEV, 0)
        win_pos = lax.dynamic_slice_in_dim(key_pos, row_start, window_rows, 0)
        win_seg = lax.dynamic_slice_in_dim(key_seg, row_start, window_rows, 0)
        allowed = (query_seg[:, None] == win_seg[None, :]) & (win_pos[None, :] <= query_pos[:, None])
        scores = jnp.einsum('qhgd,khd->hgqk', query_blk, key_win) * score_scale
        scores = jnp.where(allowed, scores, -1e30)
        row_max = jnp.max(scores, axis=-1, keepdims=True)
        weights = jnp.where(allowed, jnp.exp(scores - row_max), 0.0)
        probs = weights / jnp.sum(weights, axis=-1, keepdims=True)
        probs_low = lax.optimization_barrier(probs.astype(jnp.bfloat16)).astype(jnp.float32)
        output = jnp.einsum('hgqk,khd->qhgd', probs_low, value_win)
        row_delta = jnp.transpose(jnp.sum(grad_blk * output, axis=-1), (1, 2, 0))
        grad_probs = jnp.einsum('qhgd,khd->hgqk', grad_blk, value_win)
        grad_scores = probs * (grad_probs - row_delta[..., None])
        grad_scores = lax.optimization_barrier(grad_scores.astype(jnp.bfloat16)).astype(jnp.float32)
        value_part = jnp.einsum('hgqk,qhgd->khd', probs_low, grad_blk)
        key_part = score_scale * jnp.einsum('hgqk,qhgd->khd', grad_scores, query_blk)
        query_acc = query_acc + score_scale * jnp.einsum('hgqk,khd->hgd', grad_scores, key_win)
        key_part = lax.optimization_barrier(key_part.astype(jnp.bfloat16)).astype(jnp.float32)
        value_part = lax.optimization_barrier(value_part.astype(jnp.bfloat16)).astype(jnp.float32)
        key_acc = lax.dynamic_update_slice_in_dim(
            key_acc, lax.dynamic_slice_in_dim(key_acc, row_start, window_rows, 0) + key_part, row_start, 0)
        value_acc = lax.dynamic_update_slice_in_dim(
            value_acc, lax.dynamic_slice_in_dim(value_acc, row_start, window_rows, 0) + value_part, row_start, 0)
        return (key_acc, value_acc, query_acc), None

    start_state = (jnp.zeros((SEQ + padding, KV_HEADS, HEAD_DIM), jnp.float32),
                   jnp.zeros((SEQ + padding, KV_HEADS, HEAD_DIM), jnp.float32),
                   jnp.zeros((KV_HEADS, groups, HEAD_DIM), jnp.float32))
    (key_acc, value_acc, query_acc), _ = lax.scan(block_step, start_state,
                                                  jnp.arange(SEQ // TOK_DEV, dtype=jnp.int32))
    key_sum = key_acc[padding:]
    value_sum = value_acc[padding:]
    query_bias = query_acc.reshape(-1)
    value_bias = jnp.sum(value_sum, axis=0).reshape(-1)
    key_grad = key_sum.astype(jnp.bfloat16).reshape(SEQ, KV_HEADS * HEAD_DIM)
    value_grad = value_sum.astype(jnp.bfloat16).reshape(SEQ, KV_HEADS * HEAD_DIM)
    return (key_grad, value_grad, query_bias, value_bias)
```

```python
import functools

import jax
import jax.numpy as jnp
from jax import lax
from jax.experimental import pallas as pl
from jax.experimental.pallas import tpu as pltpu
from jax.sharding import PartitionSpec as P

HEAD_DIM = 128
Q_HEADS = 32
KV_HEADS = 4
GROUP = Q_HEADS // KV_HEADS
AXES = ("dp", "ctx")
SCALE = HEAD_DIM ** (-0.5)
LOG2E = 1.4426950408889634
NT = (((1,), (1,)), ((), ()))
TN = (((0,), (0,)), ((), ()))
NN = (((1,), (0,)), ((), ()))


def dot(a, b, dims):
    return lax.dot_general(a, b, dims, preferred_element_type=jnp.float32)


def attend_kernel(reach, start_ref, q_ref, c_ref, k_ref, v_ref, *refs):
    kp_refs, vp_refs = refs[:reach], refs[reach : 2 * reach]
    own_ref, *back_refs = refs[2 * reach : 3 * reach + 1]
    bias_ref, p_ref, g_ref = refs[3 * reach + 1 :]
    rows = q_ref.shape[0]
    wide = 2 * rows
    kv_feat = k_ref.shape[1]
    key_row = lax.broadcasted_iota(jnp.int32, (rows, wide), 0)
    query_col = lax.broadcasted_iota(jnp.int32, (rows, wide), 1) & (rows - 1)
    start = start_ref[...]
    start = jnp.concatenate([start, start], axis=1)
    near = key_row <= query_col
    folded = jnp.where(near, key_row, key_row - reach * rows)
    valids = [folded >= start] + [key_row - j * rows >= start for j in range(1, reach)]
    lane = lax.broadcasted_iota(jnp.int32, (rows, HEAD_DIM), 1)
    order = [reach] + list(range(1, reach))
    for g in range(KV_HEADS):
        cols = slice(g * HEAD_DIM, (g + 1) * HEAD_DIM)
        key_all = jnp.concatenate([k_ref[:, cols]] + [kp_refs[j - 1][:, cols] for j in order], axis=0)
        value_all = jnp.concatenate([v_ref[:, cols]] + [vp_refs[j - 1][:, cols] for j in order], axis=0)
        q_list, c_list = [], []
        for pair in range(GROUP // 2):
            heads = [g * GROUP + 2 * pair + i for i in range(2)]
            q_two = [q_ref[:, h * HEAD_DIM : (h + 1) * HEAD_DIM] for h in heads]
            c_two = [c_ref[:, h * HEAD_DIM : (h + 1) * HEAD_DIM] for h in heads]
            for i in range(2):
                indicator = jnp.where(lane == 2 * pair + i, 1.0, 0.0).astype(jnp.bfloat16)
                q_list.append(jnp.concatenate([q_two[i], indicator], axis=1))
            c_list += c_two
            s_all = dot(key_all, jnp.concatenate(q_two, axis=0), NT)
            d_all = dot(value_all, jnp.concatenate(c_two, axis=0), NT)

            def parts(whole):
                cut = [whole[i * rows : (i + 1) * rows] for i in range(reach + 1)]
                return [jnp.where(near, cut[0], cut[1])] + cut[2:]

            s_parts = [jnp.where(ok, s * (SCALE * LOG2E), -1e30) for ok, s in zip(valids, parts(s_all))]
            d_parts = parts(d_all)
            top = functools.reduce(jnp.maximum, [jnp.max(s, axis=0, keepdims=True) for s in s_parts])
            e_parts = [jnp.exp2(s - top) for s in s_parts]
            total = sum(jnp.sum(e, axis=0, keepdims=True) for e in e_parts)
            inv = 1.0 / total
            delta = inv * sum(jnp.sum(e * d, axis=0, keepdims=True) for e, d in zip(e_parts, d_parts))
            at = slice(pair * wide, (pair + 1) * wide)
            for i, (e, d) in enumerate(zip(e_parts, d_parts)):
                prob = e * inv
                grad = prob * (d - delta)
                if i == 0:
                    p_ref[:rows, at] = jnp.where(near, prob, 0.0).astype(jnp.bfloat16)
                    g_ref[:rows, at] = jnp.where(near, grad, 0.0).astype(jnp.bfloat16)
                    p_ref[rows : 2 * rows, at] = jnp.where(near, 0.0, prob).astype(jnp.bfloat16)
                    g_ref[rows : 2 * rows, at] = jnp.where(near, 0.0, grad).astype(jnp.bfloat16)
                else:
                    p_ref[(i + 1) * rows : (i + 2) * rows, at] = prob.astype(jnp.bfloat16)
                    g_ref[(i + 1) * rows : (i + 2) * rows, at] = grad.astype(jnp.bfloat16)
        value_part = dot(p_ref[...], jnp.concatenate(c_list, axis=0), NN)
        key_wide = dot(g_ref[...], jnp.concatenate(q_list, axis=0), NN)
        key_part = (key_wide[:, :HEAD_DIM] * SCALE).astype(jnp.bfloat16)
        value_part = value_part.astype(jnp.bfloat16)
        for i, ref in enumerate([own_ref] + [back_refs[j - 1] for j in order]):
            ref[:, g * HEAD_DIM : (g + 1) * HEAD_DIM] = key_part[i * rows : (i + 1) * rows]
            ref[:, kv_feat + g * HEAD_DIM : kv_feat + (g + 1) * HEAD_DIM] = value_part[i * rows : (i + 1) * rows]
        bias_ref[Q_HEADS + g : Q_HEADS + g + 1, :] = jnp.sum(value_part.astype(jnp.float32), axis=0, keepdims=True)
        sums = key_wide[:, HEAD_DIM:] * SCALE
        high = sums.astype(jnp.bfloat16)
        low = (sums - high.astype(jnp.float32)).astype(jnp.bfloat16)
        query_bias = dot(high, key_all, TN) + dot(low, key_all, TN)
        bias_ref[g * GROUP : (g + 1) * GROUP, :] = query_bias[:GROUP]


def attend(reach, start, query, cotangent, keys, values, far_keys, far_values):
    rows = query.shape[0]
    kv_feat = keys.shape[1]
    window = (reach + 1) * rows
    block = jax.ShapeDtypeStruct((rows, 2 * kv_feat), jnp.bfloat16)
    vmem = pl.BlockSpec(memory_space=pltpu.VMEM)
    return pl.pallas_call(
        functools.partial(attend_kernel, reach),
        out_shape=[block] * (reach + 1) + [jax.ShapeDtypeStruct((Q_HEADS + KV_HEADS, HEAD_DIM), jnp.float32)],
        in_specs=[vmem] * (5 + 2 * reach),
        out_specs=[vmem] * (reach + 2),
        scratch_shapes=[
            pltpu.VMEM((window, GROUP * rows), jnp.bfloat16),
            pltpu.VMEM((window, GROUP * rows), jnp.bfloat16),
        ],
        compiler_params=pltpu.CompilerParams(vmem_limit_bytes=32 * 1024 * 1024),
        cost_estimate=pl.CostEstimate(flops=2 * 4 * window * rows * Q_HEADS * HEAD_DIM, bytes_accessed=3 << 20, transcendentals=window * rows * Q_HEADS),
    )(start, query, cotangent, keys, values, *far_keys, *far_values)


def shift(array, count, by):
    return lax.ppermute(array, AXES, [(i, (i + by) % count) for i in range(count)])


def all_sum(array, count):
    step = 1
    steps = []
    while step < count:
        steps.append(step)
        step *= 2
    for step in steps:
        array = array + lax.ppermute(array, AXES, [(i, i ^ step) for i in range(count)])
    return array


def body(query, keys, values, cotangent, doc_lengths):
    rows = query.shape[0]
    kv_feat = keys.shape[1]
    count = lax.axis_size("dp") * lax.axis_size("ctx")
    reach = lax.axis_size("ctx") // 4
    device = lax.axis_index(AXES)
    far_keys = [shift(keys, count, distance) for distance in range(1, reach + 1)]
    far_values = [shift(values, count, distance) for distance in range(1, reach + 1)]
    ends = jnp.cumsum(doc_lengths)
    position = device * rows + jnp.arange(rows, dtype=jnp.int32)
    start = jnp.max(jnp.where(ends[:, None] <= position[None, :], ends[:, None], 0), axis=0)
    start = (start - device * rows)[None, :]
    own, *rest = attend(reach, start, query, cotangent, keys, values, far_keys, far_values)
    *backs, bias = rest
    bias = all_sum(bias, count)
    received = own.astype(jnp.float32)
    for distance in range(1, reach + 1):
        received = received + shift(backs[distance - 1], count, -distance).astype(jnp.float32)
    received = received.astype(jnp.bfloat16)
    query_bias = bias[:Q_HEADS].reshape(-1)
    value_bias = bias[Q_HEADS:].reshape(-1)
    return (received[:, :kv_feat], received[:, kv_feat:], query_bias, value_bias)


def solution(mesh):
    return jax.shard_map(
        body,
        mesh=mesh,
        in_specs=(P(AXES, None),) * 4 + (P(),),
        out_specs=(P(AXES, None), P(AXES, None), P(), P()),
        check_vma=False,
    )
```

```python
import functools

import jax
import jax.numpy as jnp
from jax import lax
from jax.experimental import pallas as pl
from jax.experimental.pallas import tpu as pltpu
from jax.sharding import PartitionSpec as P

HEAD_DIM = 128
Q_HEADS = 32
KV_HEADS = 4
GROUP = Q_HEADS // KV_HEADS
AXES = ("dp", "ctx")
SCALE = HEAD_DIM ** (-0.5)
LOG2E = 1.4426950408889634
NT = (((1,), (1,)), ((), ()))
TN = (((0,), (0,)), ((), ()))
NN = (((1,), (0,)), ((), ()))


def dot(a, b, dims):
    return lax.dot_general(a, b, dims, preferred_element_type=jnp.float32)


def head(ref, h):
    return ref[:, h * HEAD_DIM : (h + 1) * HEAD_DIM]


def spill_of(start):
    return jnp.sum(jnp.where(start < 0, 1, 0), axis=1, keepdims=True)


def grids(rows, wide):
    key_row = lax.broadcasted_iota(jnp.int32, (rows, wide), 0)
    query_col = lax.broadcasted_iota(jnp.int32, (rows, wide), 1) & (rows - 1)
    return key_row, key_row <= query_col


def near_kernel(start_ref, q_ref, c_ref, k_ref, v_ref, s_ref, d_ref, sum_ref):
    rows = q_ref.shape[0]
    key_row, near = grids(rows, 2 * rows)
    start = jnp.concatenate([start_ref[...]] * 2, axis=1)
    valid = near & (key_row >= start)
    for pair in range(Q_HEADS // 2):
        kv = 2 * pair // GROUP
        at = slice(2 * pair * rows, 2 * (pair + 1) * rows)
        q_two = jnp.concatenate([head(q_ref, 2 * pair), head(q_ref, 2 * pair + 1)], axis=0)
        c_two = jnp.concatenate([head(c_ref, 2 * pair), head(c_ref, 2 * pair + 1)], axis=0)
        s_ref[:, at] = jnp.where(valid, dot(head(k_ref, kv), q_two, NT) * (SCALE * LOG2E), -1e30)
        d_ref[:, at] = dot(head(v_ref, kv), c_two, NT)
    for g in range(KV_HEADS):
        heads = range(g * GROUP, (g + 1) * GROUP)
        total = sum(head(c_ref, h).astype(jnp.float32) for h in heads)
        sum_ref[g : g + 1, :] = jnp.sum(total, axis=0, keepdims=True)


def far_kernel(reach, start_ref, k_ref, q_ref, c_ref, s_ref, d_ref, sum_ref, *refs):
    kp_refs, vp_refs = refs[:reach], refs[reach : 2 * reach]
    bias_ref, p_ref, g_ref = refs[2 * reach :]
    rows = q_ref.shape[0]
    wide = 2 * rows
    key_row, near = grids(rows, wide)
    start = jnp.concatenate([start_ref[...]] * 2, axis=1)
    far = jnp.logical_not(near) & (key_row - reach * rows >= start)
    valids = [key_row - j * rows >= start for j in range(1, reach)]
    order = [reach] + list(range(1, reach))
    spill = spill_of(start_ref[...])
    lane = lax.broadcasted_iota(jnp.int32, (rows, HEAD_DIM), 1)
    row = lax.broadcasted_iota(jnp.int32, (rows, HEAD_DIM), 0)
    spilled = row < spill
    indicator = jnp.concatenate(
        [jnp.where(lane == jnp.where(spilled, i, i + GROUP), 1.0, 0.0).astype(jnp.bfloat16) for i in range(GROUP)], axis=0)
    far_sum = jnp.logical_not(spilled) & (lane < GROUP)
    bias_ref[Q_HEADS:, :] = sum_ref[:KV_HEADS]
    for g in range(KV_HEADS):
        far_key = jnp.concatenate([head(kp_refs[j - 1], g) for j in order], axis=0)
        far_value = jnp.concatenate([head(vp_refs[j - 1], g) for j in order], axis=0)
        for pair in range(GROUP // 2):
            first = g * GROUP + 2 * pair
            at = slice(first * rows, (first + 2) * rows)
            q_two = jnp.concatenate([head(q_ref, first), head(q_ref, first + 1)], axis=0)
            c_two = jnp.concatenate([head(c_ref, first), head(c_ref, first + 1)], axis=0)
            s_far = dot(far_key, q_two, NT)
            d_far = dot(far_value, c_two, NT)
            cut = [slice(i * rows, (i + 1) * rows) for i in range(reach)]
            s_parts = [jnp.where(far, s_far[cut[0]] * (SCALE * LOG2E), s_ref[:, at])]
            s_parts += [jnp.where(ok, s_far[c] * (SCALE * LOG2E), -1e30) for ok, c in zip(valids, cut[1:])]
            d_parts = [jnp.where(near, d_ref[:, at], d_far[cut[0]])] + [d_far[c] for c in cut[1:]]
            top = functools.reduce(jnp.maximum, [jnp.max(s, axis=0, keepdims=True) for s in s_parts])
            e_parts = [jnp.exp2(s - top) for s in s_parts]
            total = sum(jnp.sum(e, axis=0, keepdims=True) for e in e_parts)
            inv = 1.0 / total
            delta = inv * sum(jnp.sum(e * d, axis=0, keepdims=True) for e, d in zip(e_parts, d_parts))
            for e, d, c in zip(e_parts, d_parts, cut):
                prob = e * inv
                p_ref[c, at] = prob.astype(jnp.bfloat16)
                g_ref[c, at] = (prob * (d - delta)).astype(jnp.bfloat16)
        sums = dot(g_ref[:, g * GROUP * rows : (g + 1) * GROUP * rows], indicator, NN) * SCALE
        own_sums = jnp.where(far_sum, 0.0, sums[:rows]).astype(jnp.bfloat16)
        far_sums = jnp.where(far_sum, sums[:rows], 0.0).astype(jnp.bfloat16)
        if reach > 1:
            far_sums = jnp.concatenate([far_sums, sums[rows:].astype(jnp.bfloat16)], axis=0)
        query_bias = dot(own_sums, head(k_ref, g), TN) + dot(far_sums, far_key, TN)
        bias_ref[g * GROUP : (g + 1) * GROUP, :] = query_bias[:GROUP] + query_bias[GROUP : 2 * GROUP]


def grad_kernel(reach, start_ref, q_ref, c_ref, p_ref, g_ref, own_ref, *back_refs):
    rows = q_ref.shape[0]
    kv_feat = KV_HEADS * HEAD_DIM
    order = [reach] + list(range(1, reach))
    spilled = lax.broadcasted_iota(jnp.int32, (rows, HEAD_DIM), 0) < spill_of(start_ref[...])
    low = jnp.where(spilled, 1.0, 0.0).astype(jnp.bfloat16)
    high = jnp.where(spilled, 0.0, 1.0).astype(jnp.bfloat16)
    for g in range(KV_HEADS):
        at = slice(g * GROUP * rows, (g + 1) * GROUP * rows)
        heads = range(g * GROUP, (g + 1) * GROUP)
        for lhs_ref, rhs_ref, scale, base in ((g_ref, q_ref, SCALE, 0), (p_ref, c_ref, 1.0, kv_feat)):
            two = [jnp.concatenate([head(rhs_ref, h) * high, head(rhs_ref, h) * low], axis=1) for h in heads]
            both = dot(lhs_ref[:, at], jnp.concatenate(two, axis=0), NN) * scale
            late, early = both[:, :HEAD_DIM], both[:, HEAD_DIM:]
            to = slice(base + g * HEAD_DIM, base + (g + 1) * HEAD_DIM)
            own_ref[:, to] = (late[:rows] + jnp.where(spilled, early[:rows], 0.0)).astype(jnp.bfloat16)
            back_refs[reach - 1][:, to] = jnp.where(spilled, 0.0, early[:rows]).astype(jnp.bfloat16)
            for i, j in enumerate(order[1:], 1):
                back_refs[j - 1][:, to] = (late + early)[i * rows : (i + 1) * rows].astype(jnp.bfloat16)


def call(kernel, args, outs, flops, scratch=()):
    vmem = pl.BlockSpec(memory_space=pltpu.VMEM)
    return pl.pallas_call(
        kernel,
        out_shape=[jax.ShapeDtypeStruct(*out) for out in outs],
        in_specs=[vmem] * len(args),
        out_specs=[vmem] * len(outs),
        scratch_shapes=scratch,
        compiler_params=pltpu.CompilerParams(vmem_limit_bytes=32 * 1024 * 1024),
        cost_estimate=pl.CostEstimate(flops=flops, bytes_accessed=2 << 20, transcendentals=0),
    )(*args)


def attend(reach, start, query, cotangent, keys, values, far_keys, far_values):
    rows = query.shape[0]
    kv_feat = keys.shape[1]
    unit = 2 * rows * rows * Q_HEADS * HEAD_DIM
    square = ((rows, Q_HEADS * rows), jnp.float32)
    slots = ((reach * rows, Q_HEADS * rows), jnp.bfloat16)
    block = ((rows, 2 * kv_feat), jnp.bfloat16)
    near = call(near_kernel, (start, query, cotangent, keys, values), [square, square, ((8, HEAD_DIM), jnp.float32)], 2 * unit)
    bias, probs, grads = call(
        functools.partial(far_kernel, reach),
        (start, keys, query, cotangent, *near, *far_keys, *far_values),
        [((Q_HEADS + KV_HEADS, HEAD_DIM), jnp.float32), slots, slots],
        3 * reach * unit,
    )
    own, *backs = call(
        functools.partial(grad_kernel, reach), (start, query, cotangent, probs, grads), [block] * (reach + 1), 2 * reach * unit
    )
    return own, *backs, bias


def shift(array, count, by):
    return lax.ppermute(array, AXES, [(i, (i + by) % count) for i in range(count)])


def stages(count, ctx):
    powers = [1 << i for i in range(count.bit_length() - 1)]
    return [ctx] + [p ^ ctx for p in powers if p > ctx] + [p ^ ctx for p in powers if p < ctx]


def exchange(array, step, count):
    return array + lax.ppermute(array, AXES, [(i, i ^ step) for i in range(count)])


def body(query, keys, values, cotangent, doc_lengths):
    rows = query.shape[0]
    kv_feat = keys.shape[1]
    count = lax.axis_size("dp") * lax.axis_size("ctx")
    reach = lax.axis_size("ctx") // 4
    device = lax.axis_index(AXES)
    far_keys = [shift(keys, count, distance) for distance in range(1, reach + 1)]
    far_values = [shift(values, count, distance) for distance in range(1, reach + 1)]
    ends = jnp.cumsum(doc_lengths)
    position = device * rows + jnp.arange(rows, dtype=jnp.int32)
    start = jnp.max(jnp.where(ends[:, None] <= position[None, :], ends[:, None], 0), axis=0)
    start = (start - device * rows)[None, :]
    own, *rest = attend(reach, start, query, cotangent, keys, values, far_keys, far_values)
    *backs, bias = rest
    received = own.astype(jnp.float32)
    for distance in range(1, reach + 1):
        received = received + shift(backs[distance - 1], count, -distance).astype(jnp.float32)
    received = received.astype(jnp.bfloat16)
    steps = stages(count, lax.axis_size("ctx"))
    for i, step in enumerate(steps):
        if i == len(steps) - 1:
            received, bias = lax.optimization_barrier((received, bias))
        bias = exchange(bias, step, count)
    query_bias = bias[:Q_HEADS].reshape(-1)
    value_bias = bias[Q_HEADS:].reshape(-1)
    return (received[:, :kv_feat], received[:, kv_feat:], query_bias, value_bias)


def solution(mesh):
    return jax.shard_map(
        body,
        mesh=mesh,
        in_specs=(P(AXES, None),) * 4 + (P(),),
        out_specs=(P(AXES, None), P(AXES, None), P(), P()),
        check_vma=False,
    )
```

```python
import functools

import jax
import jax.numpy as jnp
from jax import lax
from jax.experimental import pallas as pl
from jax.experimental.pallas import tpu as pltpu
from jax.sharding import PartitionSpec as P

HEAD_DIM = 128
Q_HEADS = 32
KV_HEADS = 4
GROUP = Q_HEADS // KV_HEADS
AXES = ("dp", "ctx")
SCALE = HEAD_DIM ** (-0.5)
LOG2E = 1.4426950408889634
NT = (((1,), (1,)), ((), ()))
TN = (((0,), (0,)), ((), ()))
NN = (((1,), (0,)), ((), ()))


def dot(a, b, dims):
    return lax.dot_general(a, b, dims, preferred_element_type=jnp.float32)


def head(ref, h):
    return ref[:, h * HEAD_DIM : (h + 1) * HEAD_DIM]


def spill_of(start):
    return jnp.sum(jnp.where(start < 0, 1, 0), axis=1, keepdims=True)


def grids(rows, wide):
    key_row = lax.broadcasted_iota(jnp.int32, (rows, wide), 0)
    query_col = lax.broadcasted_iota(jnp.int32, (rows, wide), 1) & (rows - 1)
    return key_row, key_row <= query_col


def near_kernel(start_ref, q_ref, c_ref, k_ref, v_ref, s_ref, d_ref, sum_ref):
    rows = q_ref.shape[0]
    key_row, near = grids(rows, 2 * rows)
    start = jnp.concatenate([start_ref[...]] * 2, axis=1)
    valid = near & (key_row >= start)
    for pair in range(Q_HEADS // 2):
        kv = 2 * pair // GROUP
        at = slice(2 * pair * rows, 2 * (pair + 1) * rows)
        q_two = jnp.concatenate([head(q_ref, 2 * pair), head(q_ref, 2 * pair + 1)], axis=0)
        c_two = jnp.concatenate([head(c_ref, 2 * pair), head(c_ref, 2 * pair + 1)], axis=0)
        s_ref[:, at] = jnp.where(valid, dot(head(k_ref, kv), q_two, NT) * (SCALE * LOG2E), -1e30)
        d_ref[:, at] = dot(head(v_ref, kv), c_two, NT)
    for g in range(KV_HEADS):
        heads = range(g * GROUP, (g + 1) * GROUP)
        total = sum(head(c_ref, h).astype(jnp.float32) for h in heads)
        sum_ref[g : g + 1, :] = jnp.sum(total, axis=0, keepdims=True)


def far_kernel(reach, start_ref, k_ref, q_ref, c_ref, s_ref, d_ref, sum_ref, *refs):
    *far_refs, bias_ref, p_ref, g_ref = refs
    kp_refs, vp_refs = far_refs[::2], far_refs[1::2]
    rows = q_ref.shape[0]
    wide = 2 * rows
    key_row, near = grids(rows, wide)
    start = jnp.concatenate([start_ref[...]] * 2, axis=1)
    far = jnp.logical_not(near) & (key_row - reach * rows >= start)
    valids = [key_row - j * rows >= start for j in range(1, reach)]
    order = [reach] + list(range(1, reach))
    spill = spill_of(start_ref[...])
    lane = lax.broadcasted_iota(jnp.int32, (rows, HEAD_DIM), 1)
    row = lax.broadcasted_iota(jnp.int32, (rows, HEAD_DIM), 0)
    spilled = row < spill
    indicator = jnp.concatenate(
        [jnp.where(lane == jnp.where(spilled, i, i + GROUP), 1.0, 0.0).astype(jnp.bfloat16) for i in range(GROUP)], axis=0)
    far_sum = jnp.logical_not(spilled) & (lane < GROUP)
    bias_ref[Q_HEADS:, :] = sum_ref[:KV_HEADS]
    for g in range(KV_HEADS):
        far_key = jnp.concatenate([head(kp_refs[j - 1], g) for j in order], axis=0)
        far_value = jnp.concatenate([head(vp_refs[j - 1], g) for j in order], axis=0)
        for pair in range(GROUP // 2):
            first = g * GROUP + 2 * pair
            at = slice(first * rows, (first + 2) * rows)
            q_two = jnp.concatenate([head(q_ref, first), head(q_ref, first + 1)], axis=0)
            c_two = jnp.concatenate([head(c_ref, first), head(c_ref, first + 1)], axis=0)
            s_far = dot(far_key, q_two, NT)
            d_far = dot(far_value, c_two, NT)
            cut = [slice(i * rows, (i + 1) * rows) for i in range(reach)]
            s_parts = [jnp.where(far, s_far[cut[0]] * (SCALE * LOG2E), s_ref[:, at])]
            s_parts += [jnp.where(ok, s_far[c] * (SCALE * LOG2E), -1e30) for ok, c in zip(valids, cut[1:])]
            d_parts = [jnp.where(near, d_ref[:, at], d_far[cut[0]])] + [d_far[c] for c in cut[1:]]
            top = functools.reduce(jnp.maximum, [jnp.max(s, axis=0, keepdims=True) for s in s_parts])
            e_parts = [jnp.exp2(s - top) for s in s_parts]
            total = sum(jnp.sum(e, axis=0, keepdims=True) for e in e_parts)
            inv = 1.0 / total
            delta = inv * sum(jnp.sum(e * d, axis=0, keepdims=True) for e, d in zip(e_parts, d_parts))
            for e, d, c in zip(e_parts, d_parts, cut):
                prob = e * inv
                p_ref[c, at] = prob.astype(jnp.bfloat16)
                g_ref[c, at] = (prob * (d - delta)).astype(jnp.bfloat16)
        sums = dot(g_ref[:, g * GROUP * rows : (g + 1) * GROUP * rows], indicator, NN) * SCALE
        own_sums = jnp.where(far_sum, 0.0, sums[:rows]).astype(jnp.bfloat16)
        far_sums = jnp.where(far_sum, sums[:rows], 0.0).astype(jnp.bfloat16)
        if reach > 1:
            far_sums = jnp.concatenate([far_sums, sums[rows:].astype(jnp.bfloat16)], axis=0)
        query_bias = dot(own_sums, head(k_ref, g), TN) + dot(far_sums, far_key, TN)
        bias_ref[g * GROUP : (g + 1) * GROUP, :] = query_bias[:GROUP] + query_bias[GROUP : 2 * GROUP]


def grad_kernel(reach, start_ref, q_ref, c_ref, p_ref, g_ref, own_ref, *back_refs):
    rows = q_ref.shape[0]
    kv_feat = KV_HEADS * HEAD_DIM
    order = [reach] + list(range(1, reach))
    spilled = lax.broadcasted_iota(jnp.int32, (rows, HEAD_DIM), 0) < spill_of(start_ref[...])
    low = jnp.where(spilled, 1.0, 0.0).astype(jnp.bfloat16)
    high = jnp.where(spilled, 0.0, 1.0).astype(jnp.bfloat16)
    for g in range(KV_HEADS):
        at = slice(g * GROUP * rows, (g + 1) * GROUP * rows)
        heads = range(g * GROUP, (g + 1) * GROUP)
        for lhs_ref, rhs_ref, scale, base in ((g_ref, q_ref, SCALE, 0), (p_ref, c_ref, 1.0, kv_feat)):
            two = [jnp.concatenate([head(rhs_ref, h) * high, head(rhs_ref, h) * low], axis=1) for h in heads]
            both = dot(lhs_ref[:, at], jnp.concatenate(two, axis=0), NN) * scale
            late, early = both[:, :HEAD_DIM], both[:, HEAD_DIM:]
            to = slice(base + g * HEAD_DIM, base + (g + 1) * HEAD_DIM)
            own_ref[:, to] = (late[:rows] + jnp.where(spilled, early[:rows], 0.0)).astype(jnp.bfloat16)
            back_refs[reach - 1][:, to] = jnp.where(spilled, 0.0, early[:rows]).astype(jnp.bfloat16)
            for i, j in enumerate(order[1:], 1):
                back_refs[j - 1][:, to] = (late + early)[i * rows : (i + 1) * rows].astype(jnp.bfloat16)


def call(kernel, args, outs, flops, scratch=()):
    vmem = pl.BlockSpec(memory_space=pltpu.VMEM)
    return pl.pallas_call(
        kernel,
        out_shape=[jax.ShapeDtypeStruct(*out) for out in outs],
        in_specs=[vmem] * len(args),
        out_specs=[vmem] * len(outs),
        scratch_shapes=scratch,
        compiler_params=pltpu.CompilerParams(vmem_limit_bytes=32 * 1024 * 1024),
        cost_estimate=pl.CostEstimate(flops=flops, bytes_accessed=2 << 20, transcendentals=0),
    )(*args)


def attend(reach, start, query, cotangent, keys, values, far):
    rows = query.shape[0]
    kv_feat = keys.shape[1]
    unit = 2 * rows * rows * Q_HEADS * HEAD_DIM
    square = ((rows, Q_HEADS * rows), jnp.float32)
    slots = ((reach * rows, Q_HEADS * rows), jnp.bfloat16)
    block = ((rows, 2 * kv_feat), jnp.bfloat16)
    near = call(near_kernel, (start, query, cotangent, keys, values), [square, square, ((8, HEAD_DIM), jnp.float32)], 2 * unit)
    bias, probs, grads = call(
        functools.partial(far_kernel, reach),
        (start, keys, query, cotangent, *near, *far),
        [((Q_HEADS + KV_HEADS, HEAD_DIM), jnp.float32), slots, slots],
        3 * reach * unit,
    )

    def gradients(start):
        return call(
            functools.partial(grad_kernel, reach), (start, query, cotangent, probs, grads), [block] * (reach + 1), 2 * reach * unit
        )

    return bias, gradients


def shift(array, count, by):
    return lax.ppermute(array, AXES, [(i, (i + by) % count) for i in range(count)])


EXCHANGE_FLOPS = 2360_000_000


def stages(count, ctx):
    powers = [1 << i for i in range(count.bit_length() - 1)]
    masks = [[ctx]] + [[p ^ ctx] for p in powers if p > ctx]
    inner = [p for p in powers if p < ctx]
    for i in range(0, len(inner), 2):
        pair = inner[i : i + 2]
        masks.append([p ^ ctx for p in pair] + ([pair[0] ^ pair[1] ^ ctx] if len(pair) > 1 else []))
    return masks


def exchange(array, masks, count):
    got = [lax.ppermute(array, AXES, [(i, i ^ mask) for i in range(count)]) for mask in masks]
    return [array] + got


def total_of(terms):
    while len(terms) > 1:
        terms = [functools.reduce(jnp.add, terms[i : i + 2]) for i in range(0, len(terms), 2)]
    return terms[0]


def add_kernel(*refs):
    *term_refs, out_ref = refs
    out_ref[...] = total_of([ref[...] for ref in term_refs])


def add(terms):
    return call(add_kernel, terms, [(terms[0].shape, terms[0].dtype)], EXCHANGE_FLOPS)[0]


def last_kernel(n_terms, n_parts, *refs):
    term_refs, part_refs = refs[:n_terms], refs[n_terms : n_terms + n_parts]
    outs, bufs, sems = refs[n_terms + n_parts : -5], refs[-5:-1], refs[-1]
    total = total_of([ref[...] for ref in term_refs])
    kv_feat = bufs[2].shape[1]
    copies = [pltpu.make_async_copy(bufs[i], outs[i], sems.at[i]) for i in range(4)]
    bufs[0][...] = total[:Q_HEADS]
    copies[0].start()
    bufs[1][...] = total[Q_HEADS:]
    copies[1].start()
    for i in range(2):
        cols = slice(i * kv_feat, (i + 1) * kv_feat)
        grad = functools.reduce(jnp.add, [ref[:, cols].astype(jnp.float32) for ref in part_refs])
        bufs[2 + i][...] = grad.astype(jnp.bfloat16)
        copies[2 + i].start()
    for copy in copies:
        copy.wait()


def last(terms, parts):
    rows, feat = parts[0].shape
    shapes = [((Q_HEADS, HEAD_DIM), jnp.float32), ((KV_HEADS, HEAD_DIM), jnp.float32)] + [((rows, feat // 2), jnp.bfloat16)] * 2
    return pl.pallas_call(
        functools.partial(last_kernel, len(terms), len(parts)),
        out_shape=[jax.ShapeDtypeStruct(*shape) for shape in shapes],
        in_specs=[pl.BlockSpec(memory_space=pltpu.VMEM)] * (len(terms) + len(parts)),
        out_specs=[pl.BlockSpec(memory_space=pl.ANY)] * 4,
        scratch_shapes=[pltpu.VMEM(*shape) for shape in shapes] + [pltpu.SemaphoreType.DMA((4,))],
        compiler_params=pltpu.CompilerParams(vmem_limit_bytes=8 * 1024 * 1024),
    )(*terms, *parts)


def body(query, keys, values, cotangent, doc_lengths):
    rows = query.shape[0]
    kv_feat = keys.shape[1]
    count = lax.axis_size("dp") * lax.axis_size("ctx")
    reach = lax.axis_size("ctx") // 4
    device = lax.axis_index(AXES)
    far = [shift(x, count, distance) for distance in range(1, reach + 1) for x in (keys, values)]
    ends = jnp.cumsum(doc_lengths)
    position = device * rows + jnp.arange(rows, dtype=jnp.int32)
    start = jnp.max(jnp.where(ends[:, None] <= position[None, :], ends[:, None], 0), axis=0)
    start = (start - device * rows)[None, :]
    bias, gradients = attend(reach, start, query, cotangent, keys, values, far)
    steps = stages(count, lax.axis_size("ctx"))
    parts = None
    for i, masks in enumerate(steps):
        if i == 1:
            start, bias = lax.optimization_barrier((start, bias))
            own, *backs = gradients(start)
            parts = [own] + [shift(backs[distance - 1], count, -distance) for distance in range(1, reach + 1)]
        terms = exchange(bias, masks, count)
        bias = add(terms) if i == 2 else total_of(terms)
    query_bias, value_bias, key_grad, value_grad = last(terms, parts)
    return (key_grad, value_grad, query_bias.reshape(-1), value_bias.reshape(-1))


def solution(mesh):
    return jax.shard_map(
        body,
        mesh=mesh,
        in_specs=(P(AXES, None),) * 4 + (P(),),
        out_specs=(P(AXES, None), P(AXES, None), P(), P()),
        check_vma=False,
    )
```

```python
import functools

import jax
import jax.numpy as jnp
from jax import lax
from jax.experimental import pallas as pl
from jax.experimental.pallas import tpu as pltpu
from jax.sharding import PartitionSpec as P

HEAD_DIM = 128
Q_HEADS = 32
KV_HEADS = 4
GROUP = Q_HEADS // KV_HEADS
AXES = ("dp", "ctx")
SCALE = HEAD_DIM ** (-0.5)
LOG2E = 1.4426950408889634
NT = (((1,), (1,)), ((), ()))
TN = (((0,), (0,)), ((), ()))
NN = (((1,), (0,)), ((), ()))


def dot(a, b, dims):
    return lax.dot_general(a, b, dims, preferred_element_type=jnp.float32)


def head(ref, h):
    return ref[:, h * HEAD_DIM : (h + 1) * HEAD_DIM]


def spill_of(start):
    return jnp.sum(jnp.where(start < 0, 1, 0), axis=1, keepdims=True)


def grids(rows, wide):
    key_row = lax.broadcasted_iota(jnp.int32, (rows, wide), 0)
    query_col = lax.broadcasted_iota(jnp.int32, (rows, wide), 1) & (rows - 1)
    return key_row, key_row <= query_col


def start_kernel(base_ref, lengths_ref, start_ref):
    docs, rows = lengths_ref.shape[1], start_ref.shape[1]
    upto = lax.broadcasted_iota(jnp.int32, (docs, docs), 1) <= lax.broadcasted_iota(jnp.int32, (docs, docs), 0)
    ends = jnp.sum(jnp.where(upto, lengths_ref[...], 0), axis=1, keepdims=True)
    base = base_ref[0]
    position = base + lax.broadcasted_iota(jnp.int32, (docs, rows), 1)
    start_ref[...] = jnp.max(jnp.where(ends <= position, ends, 0), axis=0, keepdims=True) - base


def near_kernel(start_ref, q_ref, c_ref, k_ref, v_ref, s_ref, d_ref, sum_ref):
    rows = q_ref.shape[0]
    key_row, near = grids(rows, 2 * rows)
    start = jnp.concatenate([start_ref[...]] * 2, axis=1)
    valid = near & (key_row >= start)
    for pair in range(Q_HEADS // 2):
        kv = 2 * pair // GROUP
        at = slice(2 * pair * rows, 2 * (pair + 1) * rows)
        q_two = jnp.concatenate([head(q_ref, 2 * pair), head(q_ref, 2 * pair + 1)], axis=0)
        c_two = jnp.concatenate([head(c_ref, 2 * pair), head(c_ref, 2 * pair + 1)], axis=0)
        s_ref[:, at] = jnp.where(valid, dot(head(k_ref, kv), q_two, NT) * (SCALE * LOG2E), -1e30)
        d_ref[:, at] = dot(head(v_ref, kv), c_two, NT)
    for g in range(KV_HEADS):
        heads = range(g * GROUP, (g + 1) * GROUP)
        total = sum(head(c_ref, h).astype(jnp.float32) for h in heads)
        sum_ref[g : g + 1, :] = jnp.sum(total, axis=0, keepdims=True)


def prob_kernel(reach, start_ref, q_ref, s_ref, *refs):
    *kp_refs, p_ref, low_ref, pick_ref = refs
    rows = q_ref.shape[0]
    wide = 2 * rows
    spill = spill_of(start_ref[...])
    taken = lax.broadcasted_iota(jnp.int32, (2 * Q_HEADS, rows), 0)
    taken = taken - jnp.where(lax.broadcasted_iota(jnp.int32, (2 * Q_HEADS, rows), 1) < spill, 0, Q_HEADS)
    for h in range(Q_HEADS):
        pick_ref[:, h * rows : (h + 1) * rows] = jnp.where(taken == h, 1.0, 0.0).astype(jnp.bfloat16)
    key_row, near = grids(rows, wide)
    start = jnp.concatenate([start_ref[...]] * 2, axis=1)
    far = jnp.logical_not(near) & (key_row - reach * rows >= start)
    valids = [key_row - j * rows >= start for j in range(1, reach)]
    order = [reach] + list(range(1, reach))
    cut = [slice(i * rows, (i + 1) * rows) for i in range(reach)]
    for pair in range(Q_HEADS // 2):
        g, first = 2 * pair // GROUP, 2 * pair
        at = slice(first * rows, (first + 2) * rows)
        far_key = jnp.concatenate([head(kp_refs[j - 1], g) for j in order], axis=0)
        q_two = jnp.concatenate([head(q_ref, first), head(q_ref, first + 1)], axis=0)
        s_far = dot(far_key, q_two, NT)
        s_parts = [jnp.where(far, s_far[cut[0]] * (SCALE * LOG2E), s_ref[:, at])]
        s_parts += [jnp.where(ok, s_far[c] * (SCALE * LOG2E), -1e30) for ok, c in zip(valids, cut[1:])]
        top = functools.reduce(jnp.maximum, [jnp.max(s, axis=0, keepdims=True) for s in s_parts])
        e_parts = [jnp.exp2(s - top) for s in s_parts]
        inv = 1.0 / sum(jnp.sum(e, axis=0, keepdims=True) for e in e_parts)
        for e, c in zip(e_parts, cut):
            prob = e * inv
            p_ref[c, at] = prob
            low_ref[c, at] = prob.astype(jnp.bfloat16)


def far_kernel(reach, start_ref, k_ref, c_ref, d_ref, sum_ref, p_ref, pick_ref, *refs):
    kp_refs, vp_refs = refs[:reach], refs[reach : 2 * reach]
    bias_ref, g_ref = refs[2 * reach :]
    rows = c_ref.shape[0]
    _, near = grids(rows, 2 * rows)
    order = [reach] + list(range(1, reach))
    cut = [slice(i * rows, (i + 1) * rows) for i in range(reach)]
    bias_ref[Q_HEADS:, :] = sum_ref[:KV_HEADS]
    for g in range(KV_HEADS):
        far_value = jnp.concatenate([head(vp_refs[j - 1], g) for j in order], axis=0)
        for pair in range(GROUP // 2):
            first = g * GROUP + 2 * pair
            at = slice(first * rows, (first + 2) * rows)
            c_two = jnp.concatenate([head(c_ref, first), head(c_ref, first + 1)], axis=0)
            d_far = dot(far_value, c_two, NT)
            d_parts = [jnp.where(near, d_ref[:, at], d_far[cut[0]])] + [d_far[c] for c in cut[1:]]
            delta = sum(jnp.sum(p_ref[c, at] * d, axis=0, keepdims=True) for d, c in zip(d_parts, cut))
            for d, c in zip(d_parts, cut):
                g_ref[c, at] = (p_ref[c, at] * (d - delta)).astype(jnp.bfloat16)
    total = dot(pick_ref[...], g_ref[...], NT) * SCALE
    early, late = total[:Q_HEADS], total[Q_HEADS:]
    spilled = lax.broadcasted_iota(jnp.int32, (Q_HEADS, rows), 1) < spill_of(start_ref[...])
    own_sums = (late[:, :rows] + jnp.where(spilled, early[:, :rows], 0.0)).astype(jnp.bfloat16)
    far_sums = [jnp.where(spilled, 0.0, early[:, :rows]).astype(jnp.bfloat16)]
    far_sums += [(early + late)[:, c].astype(jnp.bfloat16) for c in cut[1:]]
    query_bias = dot(own_sums, k_ref[...], NN)
    for far_sum, j in zip(far_sums, order):
        query_bias = query_bias + dot(far_sum, kp_refs[j - 1][...], NN)
    for g in range(KV_HEADS):
        bias_ref[g * GROUP : (g + 1) * GROUP, :] = query_bias[g * GROUP : (g + 1) * GROUP, g * HEAD_DIM : (g + 1) * HEAD_DIM]


def grad_kernel(reach, start_ref, q_ref, c_ref, p_ref, g_ref, own_ref, *back_refs):
    rows = q_ref.shape[0]
    kv_feat = KV_HEADS * HEAD_DIM
    order = [reach] + list(range(1, reach))
    spilled = lax.broadcasted_iota(jnp.int32, (rows, HEAD_DIM), 0) < spill_of(start_ref[...])
    low = jnp.where(spilled, 1.0, 0.0).astype(jnp.bfloat16)
    high = jnp.where(spilled, 0.0, 1.0).astype(jnp.bfloat16)
    for g in range(KV_HEADS):
        at = slice(g * GROUP * rows, (g + 1) * GROUP * rows)
        heads = range(g * GROUP, (g + 1) * GROUP)
        for lhs_ref, rhs_ref, scale, base in ((g_ref, q_ref, SCALE, 0), (p_ref, c_ref, 1.0, kv_feat)):
            two = [jnp.concatenate([head(rhs_ref, h) * high, head(rhs_ref, h) * low], axis=1) for h in heads]
            both = dot(lhs_ref[:, at], jnp.concatenate(two, axis=0), NN) * scale
            late, early = both[:, :HEAD_DIM], both[:, HEAD_DIM:]
            to = slice(base + g * HEAD_DIM, base + (g + 1) * HEAD_DIM)
            own_ref[:, to] = (late[:rows] + jnp.where(spilled, early[:rows], 0.0)).astype(jnp.bfloat16)
            back_refs[reach - 1][:, to] = jnp.where(spilled, 0.0, early[:rows]).astype(jnp.bfloat16)
            for i, j in enumerate(order[1:], 1):
                back_refs[j - 1][:, to] = (late + early)[i * rows : (i + 1) * rows].astype(jnp.bfloat16)


def call(kernel, args, outs, flops, scratch=(), scalars=0):
    vmem = pl.BlockSpec(memory_space=pltpu.VMEM)
    return pl.pallas_call(
        kernel,
        out_shape=[jax.ShapeDtypeStruct(*out) for out in outs],
        in_specs=[pl.BlockSpec(memory_space=pltpu.SMEM)] * scalars + [vmem] * (len(args) - scalars),
        out_specs=[vmem] * len(outs),
        scratch_shapes=scratch,
        compiler_params=pltpu.CompilerParams(vmem_limit_bytes=32 * 1024 * 1024),
        cost_estimate=pl.CostEstimate(flops=flops, bytes_accessed=2 << 20, transcendentals=0),
    )(*args)


def attend(reach, start, query, cotangent, keys, values, far):
    rows = query.shape[0]
    kv_feat = keys.shape[1]
    unit = 2 * rows * rows * Q_HEADS * HEAD_DIM
    square = ((rows, Q_HEADS * rows), jnp.float32)
    slots = (reach * rows, Q_HEADS * rows)
    block = ((rows, 2 * kv_feat), jnp.bfloat16)
    near_s, near_d, sums = call(
        near_kernel, (start, query, cotangent, keys, values), [square, square, ((8, HEAD_DIM), jnp.float32)], 2 * unit
    )
    wide_probs, probs, pick = call(
        functools.partial(prob_kernel, reach),
        (start, query, near_s, *far[::2]),
        [(slots, jnp.float32), (slots, jnp.bfloat16), ((2 * Q_HEADS, Q_HEADS * rows), jnp.bfloat16)],
        reach * unit,
    )
    bias, grads = call(
        functools.partial(far_kernel, reach),
        (start, keys, cotangent, near_d, sums, wide_probs, pick, *far[::2], *far[1::2]),
        [((Q_HEADS + KV_HEADS, HEAD_DIM), jnp.float32), (slots, jnp.bfloat16)],
        2 * reach * unit,
    )

    def gradients(start):
        return call(
            functools.partial(grad_kernel, reach), (start, query, cotangent, probs, grads), [block] * (reach + 1), 2 * reach * unit
        )

    return bias, gradients


def shift(array, count, by):
    return lax.ppermute(array, AXES, [(i, (i + by) % count) for i in range(count)])


START_FLOPS = 3000_000_000
EXCHANGE_FLOPS = 2300_000_000


def stages(count, ctx):
    powers = [1 << i for i in range(count.bit_length() - 1)]
    masks = [[ctx]] + [[p ^ ctx] for p in powers if p > ctx]
    inner = [p for p in powers if p < ctx]
    for i in range(0, len(inner), 2):
        pair = inner[i : i + 2]
        masks.append([p ^ ctx for p in pair] + ([pair[0] ^ pair[1] ^ ctx] if len(pair) > 1 else []))
    return masks


def exchange(array, masks, count):
    got = [lax.ppermute(array, AXES, [(i, i ^ mask) for i in range(count)]) for mask in masks]
    return [array] + got


def total_of(terms):
    while len(terms) > 1:
        terms = [functools.reduce(jnp.add, terms[i : i + 2]) for i in range(0, len(terms), 2)]
    return terms[0]


def add_kernel(*refs):
    *term_refs, out_ref = refs
    out_ref[...] = total_of([ref[...] for ref in term_refs])


def add(terms):
    return call(add_kernel, terms, [(terms[0].shape, terms[0].dtype)], EXCHANGE_FLOPS)[0]


def last_kernel(n_terms, n_parts, *refs):
    term_refs, part_refs = refs[:n_terms], refs[n_terms : n_terms + n_parts]
    outs, bufs, sems = refs[n_terms + n_parts : -5], refs[-5:-1], refs[-1]
    total = total_of([ref[...] for ref in term_refs])
    kv_feat = bufs[2].shape[1]
    copies = [pltpu.make_async_copy(bufs[i], outs[i], sems.at[i]) for i in range(4)]
    bufs[0][...] = total[:Q_HEADS]
    copies[0].start()
    bufs[1][...] = total[Q_HEADS:]
    copies[1].start()
    for i in range(2):
        cols = slice(i * kv_feat, (i + 1) * kv_feat)
        grad = functools.reduce(jnp.add, [ref[:, cols].astype(jnp.float32) for ref in part_refs])
        bufs[2 + i][...] = grad.astype(jnp.bfloat16)
        copies[2 + i].start()
    for copy in copies:
        copy.wait()


def last(terms, parts):
    rows, feat = parts[0].shape
    shapes = [((Q_HEADS, HEAD_DIM), jnp.float32), ((KV_HEADS, HEAD_DIM), jnp.float32)] + [((rows, feat // 2), jnp.bfloat16)] * 2
    return pl.pallas_call(
        functools.partial(last_kernel, len(terms), len(parts)),
        out_shape=[jax.ShapeDtypeStruct(*shape) for shape in shapes],
        in_specs=[pl.BlockSpec(memory_space=pltpu.VMEM)] * (len(terms) + len(parts)),
        out_specs=[pl.BlockSpec(memory_space=pl.ANY)] * 4,
        scratch_shapes=[pltpu.VMEM(*shape) for shape in shapes] + [pltpu.SemaphoreType.DMA((4,))],
        compiler_params=pltpu.CompilerParams(vmem_limit_bytes=8 * 1024 * 1024),
    )(*terms, *parts)


def body(query, keys, values, cotangent, doc_lengths):
    rows = query.shape[0]
    kv_feat = keys.shape[1]
    count = lax.axis_size("dp") * lax.axis_size("ctx")
    reach = lax.axis_size("ctx") // 4
    device = lax.axis_index(AXES)
    far = [shift(x, count, distance) for distance in range(1, reach + 1) for x in (keys, values)]
    base = (device * rows).reshape(1)
    (start,) = call(start_kernel, (base, doc_lengths.reshape(1, -1)), [((1, rows), jnp.int32)], START_FLOPS, (), 1)
    bias, gradients = attend(reach, start, query, cotangent, keys, values, far)
    steps = stages(count, lax.axis_size("ctx"))
    parts = None
    for i, masks in enumerate(steps):
        if i == 1:
            start, bias = lax.optimization_barrier((start, bias))
            own, *backs = gradients(start)
            parts = [own] + [shift(backs[distance - 1], count, -distance) for distance in range(1, reach + 1)]
        terms = exchange(bias, masks, count)
        bias = add(terms) if i == 2 else total_of(terms)
    query_bias, value_bias, key_grad, value_grad = last(terms, parts)
    return (key_grad, value_grad, query_bias.reshape(-1), value_bias.reshape(-1))


def solution(mesh):
    return jax.shard_map(
        body,
        mesh=mesh,
        in_specs=(P(AXES, None),) * 4 + (P(),),
        out_specs=(P(AXES, None), P(AXES, None), P(), P()),
        check_vma=False,
    )
```

```python
import functools

import jax
import jax.numpy as jnp
from jax import lax
from jax.experimental import pallas as pl
from jax.experimental.pallas import tpu as pltpu
from jax.sharding import PartitionSpec as P

HEAD_DIM = 128
Q_HEADS = 32
KV_HEADS = 4
GROUP = Q_HEADS // KV_HEADS
AXES = ("dp", "ctx")
SCALE = HEAD_DIM ** (-0.5)
LOG2E = 1.4426950408889634
NT = (((1,), (1,)), ((), ()))
TN = (((0,), (0,)), ((), ()))
NN = (((1,), (0,)), ((), ()))


def dot(a, b, dims):
    return lax.dot_general(a, b, dims, preferred_element_type=jnp.float32)


def head(ref, h):
    return ref[:, h * HEAD_DIM : (h + 1) * HEAD_DIM]


def spill_of(start):
    return jnp.sum(jnp.where(start < 0, 1, 0), axis=1, keepdims=True)


def grids(rows, wide):
    key_row = lax.broadcasted_iota(jnp.int32, (rows, wide), 0)
    query_col = lax.broadcasted_iota(jnp.int32, (rows, wide), 1) & (rows - 1)
    return key_row, key_row <= query_col


def start_kernel(base_ref, lengths_ref, start_ref):
    docs, rows = lengths_ref.shape[1], start_ref.shape[1]
    upto = lax.broadcasted_iota(jnp.int32, (docs, docs), 1) <= lax.broadcasted_iota(jnp.int32, (docs, docs), 0)
    ends = jnp.sum(jnp.where(upto, lengths_ref[...], 0), axis=1, keepdims=True)
    base = base_ref[0]
    position = base + lax.broadcasted_iota(jnp.int32, (docs, rows), 1)
    start_ref[...] = jnp.max(jnp.where(ends <= position, ends, 0), axis=0, keepdims=True) - base


def near_kernel(start_ref, q_ref, c_ref, k_ref, v_ref, s_ref, d_ref, sum_ref):
    rows = q_ref.shape[0]
    key_row, near = grids(rows, 2 * rows)
    start = jnp.concatenate([start_ref[...]] * 2, axis=1)
    valid = near & (key_row >= start)
    for pair in range(Q_HEADS // 2):
        kv = 2 * pair // GROUP
        at = slice(2 * pair * rows, 2 * (pair + 1) * rows)
        q_two = jnp.concatenate([head(q_ref, 2 * pair), head(q_ref, 2 * pair + 1)], axis=0)
        c_two = jnp.concatenate([head(c_ref, 2 * pair), head(c_ref, 2 * pair + 1)], axis=0)
        s_ref[:, at] = jnp.where(valid, dot(head(k_ref, kv), q_two, NT) * (SCALE * LOG2E), -1e30)
        d_ref[:, at] = dot(head(v_ref, kv), c_two, NT)
    for g in range(KV_HEADS):
        heads = range(g * GROUP, (g + 1) * GROUP)
        total = sum(head(c_ref, h).astype(jnp.float32) for h in heads)
        sum_ref[g : g + 1, :] = jnp.sum(total, axis=0, keepdims=True)


def prob_kernel(reach, start_ref, q_ref, s_ref, *refs):
    *kp_refs, p_ref, low_ref, pick_ref = refs
    rows = q_ref.shape[0]
    wide = 2 * rows
    spill = spill_of(start_ref[...])
    taken = lax.broadcasted_iota(jnp.int32, (2 * Q_HEADS, rows), 0)
    taken = taken - jnp.where(lax.broadcasted_iota(jnp.int32, (2 * Q_HEADS, rows), 1) < spill, 0, Q_HEADS)
    for h in range(Q_HEADS):
        pick_ref[:, h * rows : (h + 1) * rows] = jnp.where(taken == h, 1.0, 0.0).astype(jnp.bfloat16)
    key_row, near = grids(rows, wide)
    start = jnp.concatenate([start_ref[...]] * 2, axis=1)
    far = jnp.logical_not(near) & (key_row - reach * rows >= start)
    valids = [key_row - j * rows >= start for j in range(1, reach)]
    order = [reach] + list(range(1, reach))
    cut = [slice(i * rows, (i + 1) * rows) for i in range(reach)]
    for pair in range(Q_HEADS // 2):
        g, first = 2 * pair // GROUP, 2 * pair
        at = slice(first * rows, (first + 2) * rows)
        far_key = jnp.concatenate([head(kp_refs[j - 1], g) for j in order], axis=0)
        q_two = jnp.concatenate([head(q_ref, first), head(q_ref, first + 1)], axis=0)
        s_far = dot(far_key, q_two, NT)
        s_parts = [jnp.where(far, s_far[cut[0]] * (SCALE * LOG2E), s_ref[:, at])]
        s_parts += [jnp.where(ok, s_far[c] * (SCALE * LOG2E), -1e30) for ok, c in zip(valids, cut[1:])]
        top = functools.reduce(jnp.maximum, [jnp.max(s, axis=0, keepdims=True) for s in s_parts])
        e_parts = [jnp.exp2(s - top) for s in s_parts]
        inv = 1.0 / sum(jnp.sum(e, axis=0, keepdims=True) for e in e_parts)
        for e, c in zip(e_parts, cut):
            prob = e * inv
            p_ref[c, at] = prob
            low_ref[c, at] = prob.astype(jnp.bfloat16)


def far_kernel(reach, start_ref, k_ref, c_ref, d_ref, sum_ref, p_ref, pick_ref, *refs):
    kp_refs, vp_refs = refs[:reach], refs[reach : 2 * reach]
    bias_ref, g_ref = refs[2 * reach :]
    rows = c_ref.shape[0]
    _, near = grids(rows, 2 * rows)
    order = [reach] + list(range(1, reach))
    cut = [slice(i * rows, (i + 1) * rows) for i in range(reach)]
    bias_ref[Q_HEADS:, :] = sum_ref[:KV_HEADS]
    for g in range(KV_HEADS):
        far_value = jnp.concatenate([head(vp_refs[j - 1], g) for j in order], axis=0)
        for pair in range(GROUP // 2):
            first = g * GROUP + 2 * pair
            at = slice(first * rows, (first + 2) * rows)
            c_two = jnp.concatenate([head(c_ref, first), head(c_ref, first + 1)], axis=0)
            d_far = dot(far_value, c_two, NT)
            d_parts = [jnp.where(near, d_ref[:, at], d_far[cut[0]])] + [d_far[c] for c in cut[1:]]
            delta = sum(jnp.sum(p_ref[c, at] * d, axis=0, keepdims=True) for d, c in zip(d_parts, cut))
            for d, c in zip(d_parts, cut):
                g_ref[c, at] = (p_ref[c, at] * (d - delta)).astype(jnp.bfloat16)
    total = dot(pick_ref[...], g_ref[...], NT) * SCALE
    early, late = total[:Q_HEADS], total[Q_HEADS:]
    spilled = lax.broadcasted_iota(jnp.int32, (Q_HEADS, rows), 1) < spill_of(start_ref[...])
    own_sums = (late[:, :rows] + jnp.where(spilled, early[:, :rows], 0.0)).astype(jnp.bfloat16)
    far_sums = [jnp.where(spilled, 0.0, early[:, :rows]).astype(jnp.bfloat16)]
    far_sums += [(early + late)[:, c].astype(jnp.bfloat16) for c in cut[1:]]
    query_bias = dot(own_sums, k_ref[...], NN)
    for far_sum, j in zip(far_sums, order):
        query_bias = query_bias + dot(far_sum, kp_refs[j - 1][...], NN)
    for g in range(KV_HEADS):
        bias_ref[g * GROUP : (g + 1) * GROUP, :] = query_bias[g * GROUP : (g + 1) * GROUP, g * HEAD_DIM : (g + 1) * HEAD_DIM]


def grad_kernel(reach, start_ref, q_ref, c_ref, p_ref, g_ref, own_ref, *back_refs):
    rows = q_ref.shape[0]
    kv_feat = KV_HEADS * HEAD_DIM
    order = [reach] + list(range(1, reach))
    spilled = lax.broadcasted_iota(jnp.int32, (rows, HEAD_DIM), 0) < spill_of(start_ref[...])
    low = jnp.where(spilled, 1.0, 0.0).astype(jnp.bfloat16)
    high = jnp.where(spilled, 0.0, 1.0).astype(jnp.bfloat16)
    for g in range(KV_HEADS):
        at = slice(g * GROUP * rows, (g + 1) * GROUP * rows)
        heads = range(g * GROUP, (g + 1) * GROUP)
        for lhs_ref, rhs_ref, scale, base in ((g_ref, q_ref, SCALE, 0), (p_ref, c_ref, 1.0, kv_feat)):
            two = [jnp.concatenate([head(rhs_ref, h) * high, head(rhs_ref, h) * low], axis=1) for h in heads]
            both = dot(lhs_ref[:, at], jnp.concatenate(two, axis=0), NN) * scale
            late, early = both[:, :HEAD_DIM], both[:, HEAD_DIM:]
            to = slice(base + g * HEAD_DIM, base + (g + 1) * HEAD_DIM)
            own_ref[:, to] = (late[:rows] + jnp.where(spilled, early[:rows], 0.0)).astype(jnp.bfloat16)
            back_refs[reach - 1][:, to] = jnp.where(spilled, 0.0, early[:rows]).astype(jnp.bfloat16)
            for i, j in enumerate(order[1:], 1):
                back_refs[j - 1][:, to] = (late + early)[i * rows : (i + 1) * rows].astype(jnp.bfloat16)


def call(kernel, args, outs, flops, scratch=(), scalars=0):
    vmem = pl.BlockSpec(memory_space=pltpu.VMEM)
    return pl.pallas_call(
        kernel,
        out_shape=[jax.ShapeDtypeStruct(*out) for out in outs],
        in_specs=[pl.BlockSpec(memory_space=pltpu.SMEM)] * scalars + [vmem] * (len(args) - scalars),
        out_specs=[vmem] * len(outs),
        scratch_shapes=scratch,
        compiler_params=pltpu.CompilerParams(vmem_limit_bytes=32 * 1024 * 1024),
        cost_estimate=pl.CostEstimate(flops=flops, bytes_accessed=2 << 20, transcendentals=0),
    )(*args)


def attend(reach, start, query, cotangent, keys, values, far):
    rows = query.shape[0]
    kv_feat = keys.shape[1]
    unit = 2 * rows * rows * Q_HEADS * HEAD_DIM
    square = ((rows, Q_HEADS * rows), jnp.float32)
    slots = (reach * rows, Q_HEADS * rows)
    block = ((rows, 2 * kv_feat), jnp.bfloat16)
    near_s, near_d, sums = call(
        near_kernel, (start, query, cotangent, keys, values), [square, square, ((8, HEAD_DIM), jnp.float32)], 2 * unit
    )
    wide_probs, probs, pick = call(
        functools.partial(prob_kernel, reach),
        (start, query, near_s, *far[::2]),
        [(slots, jnp.float32), (slots, jnp.bfloat16), ((2 * Q_HEADS, Q_HEADS * rows), jnp.bfloat16)],
        reach * unit,
    )
    bias, grads = call(
        functools.partial(far_kernel, reach),
        (start, keys, cotangent, near_d, sums, wide_probs, pick, *far[::2], *far[1::2]),
        [((Q_HEADS + KV_HEADS, HEAD_DIM), jnp.float32), (slots, jnp.bfloat16)],
        2 * reach * unit,
    )

    def gradients(start):
        return call(
            functools.partial(grad_kernel, reach), (start, query, cotangent, probs, grads), [block] * (reach + 1), 2 * reach * unit
        )

    return bias, gradients


def shift(array, count, by):
    return lax.ppermute(array, AXES, [(i, (i + by) % count) for i in range(count)])


START_FLOPS = 3000_000_000
EXCHANGE_FLOPS = 2300_000_000


def stages(count, ctx):
    powers = [1 << i for i in range(count.bit_length() - 1)]
    outer = [p for p in powers if p > ctx]
    inner = [p for p in powers if p < ctx]
    masks = [[ctx, outer[0] ^ ctx, outer[0]]] + [[p ^ ctx] for p in outer[1:]]
    for i in range(0, len(inner), 2):
        pair = inner[i : i + 2]
        masks.append([p ^ ctx for p in pair] + ([pair[0] ^ pair[1] ^ ctx] if len(pair) > 1 else []))
    return masks


def exchange(array, masks, count):
    got = [lax.ppermute(array, AXES, [(i, i ^ mask) for i in range(count)]) for mask in masks]
    return [array] + got


def total_of(terms):
    while len(terms) > 1:
        terms = [functools.reduce(jnp.add, terms[i : i + 2]) for i in range(0, len(terms), 2)]
    return terms[0]


def add_kernel(*refs):
    *term_refs, out_ref = refs
    out_ref[...] = total_of([ref[...] for ref in term_refs])


def add(terms):
    return call(add_kernel, terms, [(terms[0].shape, terms[0].dtype)], EXCHANGE_FLOPS)[0]


def last_kernel(n_terms, n_parts, *refs):
    term_refs, part_refs = refs[:n_terms], refs[n_terms : n_terms + n_parts]
    outs, bufs, sems = refs[n_terms + n_parts : -5], refs[-5:-1], refs[-1]
    total = total_of([ref[...] for ref in term_refs])
    kv_feat = bufs[2].shape[1]
    copies = [pltpu.make_async_copy(bufs[i], outs[i], sems.at[i]) for i in range(4)]
    bufs[0][...] = total[:Q_HEADS]
    copies[0].start()
    bufs[1][...] = total[Q_HEADS:]
    copies[1].start()
    for i in range(2):
        cols = slice(i * kv_feat, (i + 1) * kv_feat)
        grad = functools.reduce(jnp.add, [ref[:, cols].astype(jnp.float32) for ref in part_refs])
        bufs[2 + i][...] = grad.astype(jnp.bfloat16)
        copies[2 + i].start()
    for copy in copies:
        copy.wait()


def last(terms, parts):
    rows, feat = parts[0].shape
    shapes = [((Q_HEADS, HEAD_DIM), jnp.float32), ((KV_HEADS, HEAD_DIM), jnp.float32)] + [((rows, feat // 2), jnp.bfloat16)] * 2
    return pl.pallas_call(
        functools.partial(last_kernel, len(terms), len(parts)),
        out_shape=[jax.ShapeDtypeStruct(*shape) for shape in shapes],
        in_specs=[pl.BlockSpec(memory_space=pltpu.VMEM)] * (len(terms) + len(parts)),
        out_specs=[pl.BlockSpec(memory_space=pl.ANY)] * 4,
        scratch_shapes=[pltpu.VMEM(*shape) for shape in shapes] + [pltpu.SemaphoreType.DMA((4,))],
        compiler_params=pltpu.CompilerParams(vmem_limit_bytes=8 * 1024 * 1024),
    )(*terms, *parts)


def body(query, keys, values, cotangent, doc_lengths):
    rows = query.shape[0]
    kv_feat = keys.shape[1]
    count = lax.axis_size("dp") * lax.axis_size("ctx")
    reach = lax.axis_size("ctx") // 4
    device = lax.axis_index(AXES)
    far = [shift(x, count, distance) for distance in range(1, reach + 1) for x in (keys, values)]
    base = (device * rows).reshape(1)
    (start,) = call(start_kernel, (base, doc_lengths.reshape(1, -1)), [((1, rows), jnp.int32)], START_FLOPS, (), 1)
    bias, gradients = attend(reach, start, query, cotangent, keys, values, far)
    steps = stages(count, lax.axis_size("ctx"))
    own, *backs = gradients(start)
    parts = [own] + [shift(backs[distance - 1], count, -distance) for distance in range(1, reach + 1)]
    for i, masks in enumerate(steps):
        terms = exchange(bias, masks, count)
        bias = add(terms) if i == 1 else total_of(terms)
    query_bias, value_bias, key_grad, value_grad = last(terms, parts)
    return (key_grad, value_grad, query_bias.reshape(-1), value_bias.reshape(-1))


def solution(mesh):
    return jax.shard_map(
        body,
        mesh=mesh,
        in_specs=(P(AXES, None),) * 4 + (P(),),
        out_specs=(P(AXES, None), P(AXES, None), P(), P()),
        check_vma=False,
    )
```

```python
import functools

import jax
import jax.numpy as jnp
from jax import lax
from jax.experimental import pallas as pl
from jax.experimental.pallas import tpu as pltpu
from jax.sharding import PartitionSpec as P

HEAD_DIM = 128
Q_HEADS = 32
KV_HEADS = 4
GROUP = Q_HEADS // KV_HEADS
AXES = ("dp", "ctx")
SCALE = HEAD_DIM ** (-0.5)
LOG2E = 1.4426950408889634
NT = (((1,), (1,)), ((), ()))
TN = (((0,), (0,)), ((), ()))
NN = (((1,), (0,)), ((), ()))


def dot(a, b, dims):
    return lax.dot_general(a, b, dims, preferred_element_type=jnp.float32)


def head(ref, h):
    return ref[:, h * HEAD_DIM : (h + 1) * HEAD_DIM]


def spill_of(start):
    return jnp.sum(jnp.where(start < 0, 1, 0), axis=1, keepdims=True)


def grids(rows, wide):
    key_row = lax.broadcasted_iota(jnp.int32, (rows, wide), 0)
    query_col = lax.broadcasted_iota(jnp.int32, (rows, wide), 1) & (rows - 1)
    return key_row, key_row <= query_col


def start_kernel(base_ref, lengths_ref, start_ref):
    docs, rows = lengths_ref.shape[1], start_ref.shape[1]
    upto = lax.broadcasted_iota(jnp.int32, (docs, docs), 1) <= lax.broadcasted_iota(jnp.int32, (docs, docs), 0)
    ends = jnp.sum(jnp.where(upto, lengths_ref[...], 0), axis=1, keepdims=True)
    base = base_ref[0]
    position = base + lax.broadcasted_iota(jnp.int32, (docs, rows), 1)
    start_ref[...] = jnp.max(jnp.where(ends <= position, ends, 0), axis=0, keepdims=True) - base


def near_kernel(start_ref, q_ref, c_ref, k_ref, v_ref, s_ref, d_ref, sum_ref):
    rows = q_ref.shape[0]
    key_row, near = grids(rows, 2 * rows)
    start = jnp.concatenate([start_ref[...]] * 2, axis=1)
    valid = near & (key_row >= start)
    for pair in range(Q_HEADS // 2):
        kv = 2 * pair // GROUP
        at = slice(2 * pair * rows, 2 * (pair + 1) * rows)
        q_two = jnp.concatenate([head(q_ref, 2 * pair), head(q_ref, 2 * pair + 1)], axis=0)
        c_two = jnp.concatenate([head(c_ref, 2 * pair), head(c_ref, 2 * pair + 1)], axis=0)
        s_ref[:, at] = jnp.where(valid, dot(head(k_ref, kv), q_two, NT) * (SCALE * LOG2E), -1e30)
        d_ref[:, at] = dot(head(v_ref, kv), c_two, NT)
    for g in range(KV_HEADS):
        heads = range(g * GROUP, (g + 1) * GROUP)
        total = sum(head(c_ref, h).astype(jnp.float32) for h in heads)
        sum_ref[g : g + 1, :] = jnp.sum(total, axis=0, keepdims=True)


def prob_kernel(reach, start_ref, q_ref, s_ref, *refs):
    *kp_refs, p_ref, low_ref, pick_ref = refs
    rows = q_ref.shape[0]
    wide = 2 * rows
    spill = spill_of(start_ref[...])
    taken = lax.broadcasted_iota(jnp.int32, (rows, 4 * Q_HEADS), 1)
    taken = taken - jnp.where(lax.broadcasted_iota(jnp.int32, (rows, 4 * Q_HEADS), 0) < spill, 0, Q_HEADS)
    for h in range(Q_HEADS):
        pick_ref[h * rows : (h + 1) * rows, :] = jnp.where(taken == h, 1.0, 0.0).astype(jnp.bfloat16)
    key_row, near = grids(rows, wide)
    start = jnp.concatenate([start_ref[...]] * 2, axis=1)
    far = jnp.logical_not(near) & (key_row - reach * rows >= start)
    valids = [key_row - j * rows >= start for j in range(1, reach)]
    order = [reach] + list(range(1, reach))
    cut = [slice(i * rows, (i + 1) * rows) for i in range(reach)]
    for pair in range(Q_HEADS // 2):
        g, first = 2 * pair // GROUP, 2 * pair
        at = slice(first * rows, (first + 2) * rows)
        far_key = jnp.concatenate([head(kp_refs[j - 1], g) for j in order], axis=0)
        q_two = jnp.concatenate([head(q_ref, first), head(q_ref, first + 1)], axis=0)
        s_far = dot(far_key, q_two, NT)
        s_parts = [jnp.where(far, s_far[cut[0]] * (SCALE * LOG2E), s_ref[:, at])]
        s_parts += [jnp.where(ok, s_far[c] * (SCALE * LOG2E), -1e30) for ok, c in zip(valids, cut[1:])]
        top = functools.reduce(jnp.maximum, [jnp.max(s, axis=0, keepdims=True) for s in s_parts])
        e_parts = [jnp.exp2(s - top) for s in s_parts]
        inv = 1.0 / sum(jnp.sum(e, axis=0, keepdims=True) for e in e_parts)
        for e, c in zip(e_parts, cut):
            prob = e * inv
            p_ref[c, at] = prob
            low_ref[c, at] = prob.astype(jnp.bfloat16)


def far_kernel(reach, start_ref, k_ref, c_ref, d_ref, sum_ref, p_ref, pick_ref, *refs):
    kp_refs, vp_refs = refs[:reach], refs[reach : 2 * reach]
    bias_ref, g_ref = refs[2 * reach :]
    rows = c_ref.shape[0]
    _, near = grids(rows, 2 * rows)
    order = [reach] + list(range(1, reach))
    cut = [slice(i * rows, (i + 1) * rows) for i in range(reach)]
    bias_ref[Q_HEADS:, :] = sum_ref[:KV_HEADS]
    for g in range(KV_HEADS):
        far_value = jnp.concatenate([head(vp_refs[j - 1], g) for j in order], axis=0)
        for pair in range(GROUP // 2):
            first = g * GROUP + 2 * pair
            at = slice(first * rows, (first + 2) * rows)
            c_two = jnp.concatenate([head(c_ref, first), head(c_ref, first + 1)], axis=0)
            d_far = dot(far_value, c_two, NT)
            d_parts = [jnp.where(near, d_ref[:, at], d_far[cut[0]])] + [d_far[c] for c in cut[1:]]
            delta = sum(jnp.sum(p_ref[c, at] * d, axis=0, keepdims=True) for d, c in zip(d_parts, cut))
            for d, c in zip(d_parts, cut):
                g_ref[c, at] = (p_ref[c, at] * (d - delta)).astype(jnp.bfloat16)
    total = (dot(g_ref[...], pick_ref[...], NN) * SCALE).T
    early, late = total[:Q_HEADS], total[Q_HEADS : 2 * Q_HEADS]
    spilled = lax.broadcasted_iota(jnp.int32, (Q_HEADS, rows), 1) < spill_of(start_ref[...])
    own_sums = (late[:, :rows] + jnp.where(spilled, early[:, :rows], 0.0)).astype(jnp.bfloat16)
    far_sums = [jnp.where(spilled, 0.0, early[:, :rows]).astype(jnp.bfloat16)]
    far_sums += [(early + late)[:, c].astype(jnp.bfloat16) for c in cut[1:]]
    query_bias = dot(own_sums, k_ref[...], NN)
    for far_sum, j in zip(far_sums, order):
        query_bias = query_bias + dot(far_sum, kp_refs[j - 1][...], NN)
    for g in range(KV_HEADS):
        bias_ref[g * GROUP : (g + 1) * GROUP, :] = query_bias[g * GROUP : (g + 1) * GROUP, g * HEAD_DIM : (g + 1) * HEAD_DIM]


def grad_kernel(reach, start_ref, q_ref, c_ref, p_ref, g_ref, own_ref, *back_refs):
    rows = q_ref.shape[0]
    kv_feat = KV_HEADS * HEAD_DIM
    order = [reach] + list(range(1, reach))
    spilled = lax.broadcasted_iota(jnp.int32, (rows, HEAD_DIM), 0) < spill_of(start_ref[...])
    low = jnp.where(spilled, 1.0, 0.0).astype(jnp.bfloat16)
    high = jnp.where(spilled, 0.0, 1.0).astype(jnp.bfloat16)
    for g in range(KV_HEADS):
        at = slice(g * GROUP * rows, (g + 1) * GROUP * rows)
        heads = range(g * GROUP, (g + 1) * GROUP)
        for lhs_ref, rhs_ref, scale, base in ((g_ref, q_ref, SCALE, 0), (p_ref, c_ref, 1.0, kv_feat)):
            two = [jnp.concatenate([head(rhs_ref, h) * high, head(rhs_ref, h) * low], axis=1) for h in heads]
            both = dot(lhs_ref[:, at], jnp.concatenate(two, axis=0), NN) * scale
            late, early = both[:, :HEAD_DIM], both[:, HEAD_DIM:]
            to = slice(base + g * HEAD_DIM, base + (g + 1) * HEAD_DIM)
            own_ref[:, to] = (late[:rows] + jnp.where(spilled, early[:rows], 0.0)).astype(jnp.bfloat16)
            back_refs[reach - 1][:, to] = jnp.where(spilled, 0.0, early[:rows]).astype(jnp.bfloat16)
            for i, j in enumerate(order[1:], 1):
                back_refs[j - 1][:, to] = (late + early)[i * rows : (i + 1) * rows].astype(jnp.bfloat16)


def call(kernel, args, outs, flops, scratch=(), scalars=0):
    vmem = pl.BlockSpec(memory_space=pltpu.VMEM)
    return pl.pallas_call(
        kernel,
        out_shape=[jax.ShapeDtypeStruct(*out) for out in outs],
        in_specs=[pl.BlockSpec(memory_space=pltpu.SMEM)] * scalars + [vmem] * (len(args) - scalars),
        out_specs=[vmem] * len(outs),
        scratch_shapes=scratch,
        compiler_params=pltpu.CompilerParams(vmem_limit_bytes=32 * 1024 * 1024),
        cost_estimate=pl.CostEstimate(flops=flops, bytes_accessed=2 << 20, transcendentals=0),
    )(*args)


def attend(reach, start, query, cotangent, keys, values, far):
    rows = query.shape[0]
    kv_feat = keys.shape[1]
    unit = 2 * rows * rows * Q_HEADS * HEAD_DIM
    square = ((rows, Q_HEADS * rows), jnp.float32)
    slots = (reach * rows, Q_HEADS * rows)
    block = ((rows, 2 * kv_feat), jnp.bfloat16)
    near_s, near_d, sums = call(
        near_kernel, (start, query, cotangent, keys, values), [square, square, ((8, HEAD_DIM), jnp.float32)], 2 * unit
    )
    wide_probs, probs, pick = call(
        functools.partial(prob_kernel, reach),
        (start, query, near_s, *far[::2]),
        [(slots, jnp.float32), (slots, jnp.bfloat16), ((Q_HEADS * rows, 4 * Q_HEADS), jnp.bfloat16)],
        reach * unit,
    )
    bias, grads = call(
        functools.partial(far_kernel, reach),
        (start, keys, cotangent, near_d, sums, wide_probs, pick, *far[::2], *far[1::2]),
        [((Q_HEADS + KV_HEADS, HEAD_DIM), jnp.float32), (slots, jnp.bfloat16)],
        2 * reach * unit,
    )

    def gradients(start):
        return call(
            functools.partial(grad_kernel, reach), (start, query, cotangent, probs, grads), [block] * (reach + 1), 2 * reach * unit
        )

    return bias, gradients


def shift(array, count, by):
    return lax.ppermute(array, AXES, [(i, (i + by) % count) for i in range(count)])


START_FLOPS = 3000_000_000
EXCHANGE_FLOPS = 2300_000_000


def stages(count, ctx):
    powers = [1 << i for i in range(count.bit_length() - 1)]
    outer = [p for p in powers if p > ctx]
    inner = [p for p in powers if p < ctx]
    masks = [[ctx, outer[0] ^ ctx, outer[0]]] + [[p ^ ctx] for p in outer[1:]]
    for i in range(0, len(inner), 2):
        pair = inner[i : i + 2]
        masks.append([p ^ ctx for p in pair] + ([pair[0] ^ pair[1] ^ ctx] if len(pair) > 1 else []))
    return masks


def exchange(array, masks, count):
    got = [lax.ppermute(array, AXES, [(i, i ^ mask) for i in range(count)]) for mask in masks]
    return [array] + got


def total_of(terms):
    while len(terms) > 1:
        terms = [functools.reduce(jnp.add, terms[i : i + 2]) for i in range(0, len(terms), 2)]
    return terms[0]


def add_kernel(*refs):
    *term_refs, out_ref = refs
    out_ref[...] = total_of([ref[...] for ref in term_refs])


def add(terms):
    return call(add_kernel, terms, [(terms[0].shape, terms[0].dtype)], EXCHANGE_FLOPS)[0]


def last_kernel(n_terms, n_parts, *refs):
    term_refs, part_refs = refs[:n_terms], refs[n_terms : n_terms + n_parts]
    outs, bufs, sems = refs[n_terms + n_parts : -5], refs[-5:-1], refs[-1]
    total = total_of([ref[...] for ref in term_refs])
    kv_feat = bufs[2].shape[1]
    copies = [pltpu.make_async_copy(bufs[i], outs[i], sems.at[i]) for i in range(4)]
    bufs[0][...] = total[:Q_HEADS]
    copies[0].start()
    bufs[1][...] = total[Q_HEADS:]
    copies[1].start()
    for i in range(2):
        cols = slice(i * kv_feat, (i + 1) * kv_feat)
        grad = functools.reduce(jnp.add, [ref[:, cols].astype(jnp.float32) for ref in part_refs])
        bufs[2 + i][...] = grad.astype(jnp.bfloat16)
        copies[2 + i].start()
    for copy in copies:
        copy.wait()


def last(terms, parts):
    rows, feat = parts[0].shape
    shapes = [((Q_HEADS, HEAD_DIM), jnp.float32), ((KV_HEADS, HEAD_DIM), jnp.float32)] + [((rows, feat // 2), jnp.bfloat16)] * 2
    return pl.pallas_call(
        functools.partial(last_kernel, len(terms), len(parts)),
        out_shape=[jax.ShapeDtypeStruct(*shape) for shape in shapes],
        in_specs=[pl.BlockSpec(memory_space=pltpu.VMEM)] * (len(terms) + len(parts)),
        out_specs=[pl.BlockSpec(memory_space=pl.ANY)] * 4,
        scratch_shapes=[pltpu.VMEM(*shape) for shape in shapes] + [pltpu.SemaphoreType.DMA((4,))],
        compiler_params=pltpu.CompilerParams(vmem_limit_bytes=8 * 1024 * 1024),
    )(*terms, *parts)


def body(query, keys, values, cotangent, doc_lengths):
    rows = query.shape[0]
    kv_feat = keys.shape[1]
    count = lax.axis_size("dp") * lax.axis_size("ctx")
    reach = lax.axis_size("ctx") // 4
    device = lax.axis_index(AXES)
    far = [shift(x, count, distance) for distance in range(1, reach + 1) for x in (keys, values)]
    base = (device * rows).reshape(1)
    (start,) = call(start_kernel, (base, doc_lengths.reshape(1, -1)), [((1, rows), jnp.int32)], START_FLOPS, (), 1)
    bias, gradients = attend(reach, start, query, cotangent, keys, values, far)
    steps = stages(count, lax.axis_size("ctx"))
    own, *backs = gradients(start)
    parts = [own] + [shift(backs[distance - 1], count, -distance) for distance in range(1, reach + 1)]
    for i, masks in enumerate(steps):
        terms = exchange(bias, masks, count)
        bias = add(terms) if i == 1 else total_of(terms)
    query_bias, value_bias, key_grad, value_grad = last(terms, parts)
    return (key_grad, value_grad, query_bias.reshape(-1), value_bias.reshape(-1))


def solution(mesh):
    return jax.shard_map(
        body,
        mesh=mesh,
        in_specs=(P(AXES, None),) * 4 + (P(),),
        out_specs=(P(AXES, None), P(AXES, None), P(), P()),
        check_vma=False,
    )
```
